32 devices in a mesh: tm: 16 (over z, y, core), band: 2 (over x).
Axes of the slice: x: 2, y: 2, z: 4, core: 2. Of those that a mesh axis runs over, the one named last changes fastest.
Arguments:
- feats: bfloat16 [16, 16, 128, 256], P('tm', 'band'), may hold values from -6 to 6
- cotangent: bfloat16 [16, 16, 128, 256], P('tm', 'band'), may hold values from -6 to 6
- w_value: bfloat16 [256, 256], replicated, may hold values from -0.375 to 0.375
- w_logit: bfloat16 [256, 48], replicated, may hold values from -24 to 24
- w_out: bfloat16 [256, 256], replicated, may hold values from -0.375 to 0.375
- row_offsets: int32 [16, 5, 16, 128], P('tm', None, 'band'), may hold values from -1 to 0
- col_offsets: int32 [16, 5, 16, 128], P('tm', None, 'band'), may hold values from -8 to 7
- fractions: int32 [16, 2, 5, 16, 128], P('tm', None, None, 'band'), may hold values from 0 to 7
- present: int32 [16, 5], P('tm'), may hold values 0 or 1
Outputs:
- grad_feats: bfloat16 [16, 16, 128, 256], P('tm', 'band')
- grad_w_value: float32 [256, 256], replicated
- grad_w_logit: float32 [256, 48], replicated
- grad_w_out: float32 [256, 256], replicated
The draws below stay inside these ranges and needn't reach their ends.
All inputs are finite; a program needn't handle non-finite values. No bound on the sum of `present` on one device may be relied on, other than what follows from the above.
Results may differ from the reference program's by a relative error of at most 0.014.
Values may be sent and summed in bfloat16 or wider, within the bound.
A program may use at most 64 MiB of HBM per device.

```python
import jax
import jax.numpy as jnp
from jax import lax

COLS = 128
C = 256
H = 8
E = 32
K = 5
J = 6
REACH = 1
COL_REACH = 8
FRAMES = 16
NROWS = 16


def draw_w_logit(key, part):
    first = jax.random.fold_in(key, 0)
    base = jnp.clip(jax.random.normal(first, (C, H * J), jnp.float32), -6.0, 6.0) * C ** (-0.5)
    return base.astype(jnp.bfloat16)


def set_ends(drawn, rng, low, top_value):
    longest = drawn.shape.index(max(drawn.shape))
    spots = []
    for shift in (0, 1):
        where = [jax.random.randint(jax.random.fold_in(rng, axis), (), 0, length) for axis, length in enumerate(drawn.shape)]
        where[longest] = (where[longest] + shift) % drawn.shape[longest]
        spots.append(tuple(where))
    return drawn.at[spots[0]].set(low).at[spots[1]].set(top_value)


def level_of(rng, shape, pieces, least, high):
    def one(dim, blocks):
        steps = jax.random.uniform(jax.random.fold_in(jax.random.fold_in(rng, 6), dim), (blocks,), jnp.float32, least / len(pieces), high / len(pieces))
        return jnp.repeat(jnp.exp(steps), shape[dim] // blocks).reshape((-1,) + (1,) * (len(shape) - dim - 1))

    loudness = one(*pieces[0])
    for cut in pieces[1:]:
        loudness = loudness * one(*cut)
    return loudness


def scatter_about(stream_key, dims, spread, limit, cuts=(), kind=jnp.bfloat16):
    array = spread * jax.random.normal(stream_key, dims, jnp.float32)
    if cuts:
        array = array * level_of(stream_key, dims, cuts, -0.22, 0.18)
    return jnp.clip(array, -limit, limit).astype(kind)


def setup_inputs(seed: int = 0) -> dict:
    arg_keys = jax.random.split(jax.random.key(seed), 10)
    feats = scatter_about(arg_keys[0], (FRAMES, NROWS, COLS, C), 1.0, 6.0, ((0, 16), (1, 2)))
    cotangent = scatter_about(arg_keys[1], (FRAMES, NROWS, COLS, C), 1.0, 6.0, ((0, 16), (1, 2)))
    w_value = scatter_about(arg_keys[2], (C, C), C ** -0.5, 0.375)
    w_logit = draw_w_logit(jax.random.fold_in(arg_keys[9], 71), 0)
    w_out = scatter_about(arg_keys[4], (C, C), C ** -0.5, 0.375)
    row_offsets = set_ends(jax.random.randint(arg_keys[5], (FRAMES, K, NROWS, COLS), -REACH, REACH), jax.random.fold_in(arg_keys[5], 1), -REACH, REACH - 1).astype(jnp.int32)
    col_offsets = set_ends(jax.random.randint(arg_keys[6], (FRAMES, K, NROWS, COLS), -COL_REACH, COL_REACH), jax.random.fold_in(arg_keys[6], 1), -COL_REACH, COL_REACH - 1).astype(jnp.int32)
    fractions = set_ends(jax.random.randint(arg_keys[7], (FRAMES, 2, K, NROWS, COLS), 0, 8), jax.random.fold_in(arg_keys[7], 1), 0, 7).astype(jnp.int32)
    present = set_ends((jax.random.randint(arg_keys[8], (FRAMES, K), 0, 8) < 7).astype(jnp.int32), jax.random.fold_in(arg_keys[8], 1), 0, 1)
    return dict(feats=feats, cotangent=cotangent, w_value=w_value, w_logit=w_logit, w_out=w_out, row_offsets=row_offsets, col_offsets=col_offsets, fractions=fractions, present=present)


DISTANCES = (1, 2, 4, 8, 16)


def corner_list(row_shift, col_shift, row_frac, col_frac, row_here, col_here, column_count, reach_rows):
    result = []
    for row_step in (0, 1):
        if row_step == 0:
            row_weight = 8 - row_frac
        else:
            row_weight = row_frac
        for col_step in (0, 1):
            if col_step == 0:
                col_weight = 8 - col_frac
            else:
                col_weight = col_frac
            ext_row = row_here + row_shift + row_step + reach_rows
            ext_col = col_here + col_shift + col_step
            inside = (ext_col >= 0) & (ext_col < column_count)
            target = (ext_row * column_count + jnp.clip(ext_col, 0, column_count - 1)).astype(jnp.int32)
            weight = jnp.where(inside, (row_weight * col_weight).astype(jnp.float32) / 64.0, jnp.float32(0.0))
            result.append((target, weight))
    return result


def reference(feats, cotangent, w_value, w_logit, w_out, row_offsets, col_offsets, fractions, present):
    frames = feats.shape[0]
    grid_rows = feats.shape[1]
    column_count = feats.shape[2]
    channels = feats.shape[3]
    cells = grid_rows * column_count
    padded_rows = grid_rows + 2 * REACH
    flat_in = feats.reshape(frames * cells, channels)
    flat_grad = cotangent.reshape(frames * cells, channels)
    values = jnp.dot(flat_in, w_value, preferred_element_type=jnp.float32).astype(jnp.bfloat16)
    values_frames = values.reshape(frames, cells, channels)
    padded = jnp.pad(values.reshape(frames, grid_rows, column_count, channels), ((0, 0), (REACH, REACH), (0, 0), (0, 0)))
    padded = padded.reshape(frames, padded_rows * column_count, channels)
    logits_all = jnp.dot(flat_in, w_logit, preferred_element_type=jnp.float32).reshape(frames, cells, H, J)
    grad_frames = cotangent.reshape(frames, cells, channels)
    cell_index = jnp.arange(cells, dtype=jnp.int32)
    row_here = cell_index // column_count
    col_here = cell_index % column_count

    def step(accum, frame_index):
        sampled = [values_frames[frame_index]]
        corner_sets = []
        valid = [jnp.asarray(True)]
        for slot in range(K):
            distance = DISTANCES[slot]
            source = jnp.maximum(frame_index - distance, 0)
            reached = frame_index >= distance
            valid.append(reached & (present[frame_index, slot] == 1))
            block = padded[source]
            sets = corner_list(row_offsets[frame_index, slot].reshape(cells), col_offsets[frame_index, slot].reshape(cells),
                               fractions[frame_index, 0, slot].reshape(cells), fractions[frame_index, 1, slot].reshape(cells),
                               row_here, col_here, column_count, REACH)
            total = jnp.zeros((cells, channels), jnp.float32)
            for target, weight in sets:
                total = total + weight[:, None] * block[target].astype(jnp.float32)
            total = jnp.where(reached, total, jnp.float32(0.0))
            sampled.append(total.astype(jnp.bfloat16))
            corner_sets.append(sets)
        valid_vec = jnp.stack(valid)
        logits = logits_all[frame_index]
        masked = jnp.where(valid_vec[None, None, :], logits, jnp.float32(-1e30))
        top = jnp.max(masked, axis=2, keepdims=True)
        expo = jnp.where(valid_vec[None, None, :], jnp.exp(masked - top), jnp.float32(0.0))
        attn = expo / jnp.sum(expo, axis=2, keepdims=True)
        attn_low = attn.astype(jnp.bfloat16)
        stacked = jnp.stack(sampled).reshape(J, cells, H, E)
        mixed = jnp.einsum("qhj,jqhe->qhe", attn_low.astype(jnp.float32), stacked.astype(jnp.float32))
        mixed = mixed.reshape(cells, channels).astype(jnp.bfloat16)
        d_mixed = jnp.dot(grad_frames[frame_index], w_out.T, preferred_element_type=jnp.float32).astype(jnp.bfloat16)
        d_heads = d_mixed.reshape(cells, H, E).astype(jnp.float32)
        d_attn = jnp.einsum("qhe,jqhe->qhj", d_heads, stacked.astype(jnp.float32))
        d_logits = attn * (d_attn - jnp.sum(attn * d_attn, axis=2, keepdims=True))
        d_logit_low = d_logits.reshape(cells, H * J).astype(jnp.bfloat16)
        d_sampled = jnp.einsum("qhj,qhe->jqhe", attn_low.astype(jnp.float32), d_heads).astype(jnp.bfloat16)
        d_sampled = d_sampled.reshape(J, cells, channels)
        self_term = jnp.pad(d_sampled[0].astype(jnp.float32).reshape(grid_rows, column_count, channels),
                            ((REACH, REACH), (0, 0), (0, 0))).reshape(padded_rows * column_count, channels)
        accum = accum.at[frame_index].add(self_term)
        for slot in range(K):
            distance = DISTANCES[slot]
            source = jnp.maximum(frame_index - distance, 0)
            contrib = jnp.zeros((padded_rows * column_count, channels), jnp.float32)
            grad_slot = d_sampled[slot + 1].astype(jnp.float32)
            for target, weight in corner_sets[slot]:
                contrib = contrib.at[target].add(weight[:, None] * grad_slot)
            accum = accum.at[source].add(contrib)
        return accum, (mixed, d_logit_low)

    start = jnp.zeros((frames, padded_rows * column_count, channels), jnp.float32)
    accum, (mixed_all, dlog_all) = lax.scan(step, start, jnp.arange(frames, dtype=jnp.int32))
    dvalues = accum.reshape(frames, padded_rows, column_count, channels)[:, REACH:REACH + grid_rows]
    dvalues = dvalues.reshape(frames * cells, channels).astype(jnp.bfloat16)
    dlog_flat = dlog_all.reshape(frames * cells, H * J)
    grad_w_out = jnp.dot(mixed_all.reshape(frames * cells, channels).T, flat_grad, preferred_element_type=jnp.float32)
    grad_w_value = jnp.dot(flat_in.T, dvalues, preferred_element_type=jnp.float32)
    grad_w_logit = jnp.dot(flat_in.T, dlog_flat, preferred_element_type=jnp.float32)
    grad_in = flat_grad.astype(jnp.float32) + jnp.dot(dvalues, w_value.T, preferred_element_type=jnp.float32)
    grad_in = grad_in + jnp.dot(dlog_flat, w_logit.T, preferred_element_type=jnp.float32)
    grad_feats = grad_in.astype(jnp.bfloat16).reshape(feats.shape)
    return (grad_feats, grad_w_value, grad_w_logit, grad_w_out)
```

```python
import functools

import jax
import jax.numpy as jnp
from jax import lax
from jax.experimental import pallas as pl
from jax.experimental.pallas import tpu as pltpu
from jax.sharding import PartitionSpec as P

H = 8
E = 32
K = 5
J = 6
DISTANCES = (1, 2, 4, 8, 16)
CHUNK = 16
MESH = pl.DeviceIdType.MESH
F32 = jnp.float32
BF16 = jnp.bfloat16


def nt_dot(a, b):
    return lax.dot_general(a, b, (((1,), (1,)), ((), ())), preferred_element_type=F32)


def dot(a, b):
    return jnp.dot(a, b, preferred_element_type=F32)


def spread_heads(a):
    return jnp.concatenate([jnp.broadcast_to(a[h : h + 1], (E, a.shape[1])) for h in range(H)], axis=0)


def head_sums(x):
    return jnp.sum(x.reshape(H, E, x.shape[1]), axis=1)


def kernel(
    nt, nb, owners,
    feats, cot, w_value, w_value_t, w_out, wl_t, wl, row_off, col_off, frac, present,
    out_feats, out_value, out_logit, out_wout,
    val, ext, tables, attn, dmix, dattn, mix, dlog, acc, cout, cin, rim_out, rim_in,
    g_out, g_val, g_log, s_out, s_val, s_log, r_out, r_val, r_log,
    band_part, whole, gathered,
    fs, fr, hs, hr, bs, br, ms, mr, ros, ror, rvs, rvr, rls, rlr, xs, xr, gs, gr, gls, glr,
):
    t = lax.axis_index("tm")
    b = lax.axis_index("band")
    rows, cols, chans = feats.shape[1:]
    slots = [k for k in range(K) if DISTANCES[k] < nt]
    chained = 2 in slots and 3 in slots
    near, far = 2, 3
    log_chunks = (H * J) // CHUNK

    barrier = pltpu.get_barrier_semaphore()

    def greet_t(i, c):
        pl.semaphore_signal(barrier, inc=1, device_id=(lax.rem(t + i, nt), b), device_id_type=MESH)
        return c

    def greet_b(i, c):
        pl.semaphore_signal(barrier, inc=1, device_id=(t, lax.rem(b + i, nb)), device_id_type=MESH)
        return c

    lax.fori_loop(1, nt, greet_t, 0)
    lax.fori_loop(1, nb, greet_b, 0)

    def rc(src, dst, ss, rs, tt, bb):
        return pltpu.make_async_remote_copy(
            src_ref=src, dst_ref=dst, send_sem=ss, recv_sem=rs, device_id=(tt, bb), device_id_type=MESH
        )

    def loop(body):
        def step(r, c):
            body(r)
            return c

        lax.fori_loop(0, rows, step, 0)

    def make_values(r):
        val[r] = nt_dot(w_value_t[...], feats[0, r]).astype(BF16)

    loop(make_values)
    pl.semaphore_wait(barrier, nt - 1 + nb - 1)

    def hop(k):
        return DISTANCES[near] if chained and k == far else DISTANCES[k]

    def main_of(k):
        return ext.at[k, pl.ds(1, rows)]

    def fwd(k):
        src = main_of(near) if chained and k == far else val
        return rc(src, main_of(k), fs.at[k], fr.at[k], lax.rem(t + hop(k), nt), b)

    def sends_fwd(k):
        if chained and k == far:
            return (t >= DISTANCES[near]) & (t + DISTANCES[near] < nt)
        return t + DISTANCES[k] < nt

    order = [k for k in (2, 1, 0, 4) if k in slots]
    for k in order:
        @pl.when(sends_fwd(k))
        def _(k=k):
            fwd(k).start()

    def make_attn(r):
        dmix[r] = nt_dot(w_out[...], cot[0, r]).astype(BF16)
        logits = nt_dot(wl_t[...], feats[0, r])
        ls = [logits[0:H]]
        oks = [None]
        for k in slots:
            flag = present[0, k] * jnp.where(t >= DISTANCES[k], 1, 0)
            ok = jnp.full((H, cols), flag, jnp.int32) == 1
            oks.append(ok)
            ls.append(jnp.where(ok, logits[H * (k + 1) : H * (k + 2)], F32(-1e30)))
        top = functools.reduce(jnp.maximum, ls)
        es = []
        for ok, l in zip(oks, ls):
            e = jnp.exp(l - top)
            es.append(e if ok is None else jnp.where(ok, e, F32(0.0)))
        total = functools.reduce(jnp.add, es)
        for j in range(len(es)):
            attn[r, j] = es[j] / total

    loop(make_attn)

    def low(r, j):
        return spread_heads(attn[r, j].astype(BF16).astype(F32))

    def rim(k, side):
        other = b - 1 if side == 0 else b + 1
        return rc(rim_out.at[k, side], rim_in.at[k, 1 - side], ms.at[k, side], mr.at[k, 1 - side],
                  t, lax.rem(other + nb, nb))

    def has(side):
        return b > 0 if side == 0 else b < nb - 1

    def contribute(k):
        acc[k] = jnp.zeros_like(acc[k])

        def body(r):
            delta = lax.broadcasted_iota(jnp.int32, (cols, cols), 0) - lax.broadcasted_iota(jnp.int32, (cols, cols), 1)
            up = row_off[0, k, pl.ds(r, 1), :] < 0
            u = delta - col_off[0, k, pl.ds(r, 1), :]
            fa = frac[0, 0, k, pl.ds(r, 1), :].astype(F32)
            fb = frac[0, 1, k, pl.ds(r, 1), :].astype(F32)
            wc = jnp.where(u == 0, 8.0 - fb, jnp.where(u == 1, fb, F32(0.0)))
            first = (8.0 - fa) / 64.0
            second = fa / 64.0
            weights = (jnp.where(up, first, F32(0.0)), jnp.where(up, second, first), jnp.where(up, F32(0.0), second))
            table = jnp.concatenate([(wc * w).astype(BF16) for w in weights], axis=0)
            tables[k, r] = table
            ds = (low(r, k + 1) * dmix[r].astype(F32)).astype(BF16)
            part = nt_dot(ds, table)
            for d in range(3):
                acc[k, r + d] += part[:, d * cols : (d + 1) * cols]

        loop(body)
        for side in (0, 1):
            rim_out[k, side] = acc[k, 0 if side == 0 else rows + 1].astype(BF16)

            @pl.when(has(side))
            def _(side=side):
                rim(k, side).start()

    def bwd(k):
        return rc(cout.at[k], cin.at[k], bs.at[k], br.at[k], lax.rem(t - hop(k) + nt, nt), b)

    def sends_bwd(k):
        return t >= DISTANCES[k]

    def gets_bwd(k):
        if chained and k == far:
            return (t >= DISTANCES[near]) & (t + DISTANCES[near] < nt)
        return t + DISTANCES[k] < nt

    def finish_contribution(k):
        for side in (0, 1):
            @pl.when(has(side))
            def _(side=side):
                rim(k, 1 - side).wait_recv()
                row = 1 if side == 0 else rows
                acc[k, row] += rim_in[k, side].astype(F32)

        if chained and k == near:
            @pl.when(gets_bwd(far))
            def _():
                bwd(far).wait_recv()

                def body(r):
                    acc[k, r + 1] += cin[far, r].astype(F32)

                loop(body)

        def body(r):
            cout[k, r] = acc[k, r + 1].astype(BF16)

        loop(body)

        @pl.when(sends_bwd(k))
        def _():
            bwd(k).start()

    back_order = [k for k in (3, 1, 0, 2, 4) if k in slots]
    late = [near] if chained else []
    previous = None
    for k in back_order:
        contribute(k)
        if previous is not None:
            finish_contribution(previous)
        previous = None if k in late else k
    if previous is not None:
        finish_contribution(previous)

    def halo(k, side):
        src = ext.at[k, 1 if side == 0 else rows]
        dst = ext.at[k, rows + 1 if side == 0 else 0]
        other = b - 1 if side == 0 else b + 1
        return rc(src, dst, hs.at[k, side], hr.at[k, 1 - side], t, lax.rem(other + nb, nb))

    def take(k):
        @pl.when(t >= DISTANCES[k])
        def _():
            fwd(k).wait_recv()
            for side in (0, 1):
                @pl.when(has(side))
                def _(side=side):
                    halo(k, side).start()

                @pl.when(jnp.logical_not(has(side)))
                def _(side=side):
                    ext[k, 0 if side == 0 else rows + 1] = jnp.zeros((chans, cols), BF16)

        @pl.when(t < DISTANCES[k])
        def _():
            ext[k] = jnp.zeros_like(ext[k])

    def clear_mix(r):
        s = val[r].astype(F32)
        mix[r] = low(r, 0) * s
        dattn[r, 0] = head_sums(dmix[r].astype(F32) * s)

    def sample(k):
        for side in (0, 1):
            @pl.when((t >= DISTANCES[k]) & has(side))
            def _(side=side):
                halo(k, 1 - side).wait_recv()

        def body(r):
            v = jnp.concatenate([ext[k, r], ext[k, r + 1], ext[k, r + 2]], axis=1)
            s = dot(v, tables[k, r]).astype(BF16).astype(F32)
            mix[r] += low(r, k + 1) * s
            dattn[r, k + 1] = head_sums(dmix[r].astype(F32) * s)

        loop(body)

    if chained:
        take(near)

        @pl.when(sends_fwd(far))
        def _():
            fwd(far).start()

    loop(clear_mix)
    for k in order:
        if not (chained and k == near):
            take(k)
    for k in late:
        finish_contribution(k)
    for k in order:
        sample(k)
    if far in slots:
        take(far)
        sample(far)

    g_out[...] = jnp.zeros_like(g_out)
    g_val[...] = jnp.zeros_like(g_val)
    g_log[...] = jnp.zeros_like(g_log)
    used = len(slots) + 1

    def finish_attn(r):
        ats = [attn[r, j] for j in range(used)]
        das = [dattn[r, j] for j in range(used)]
        inner = functools.reduce(jnp.add, [a * d for a, d in zip(ats, das)])
        dls = [a * (d - inner) for a, d in zip(ats, das)]
        dls += [jnp.zeros((H, cols), F32)] * (J - used)
        dl = jnp.concatenate(dls, axis=0).astype(BF16)
        dlog[r] = dl
        g_log[...] += dot(dl, feats[0, r])
        g_out[...] += dot(mix[r].astype(BF16), cot[0, r])

    loop(finish_attn)

    def peers(body):
        def step(i, c):
            body(lax.rem(t + i, nt))
            return c

        lax.fori_loop(1, nt, step, 0)

    def part(o):
        return pl.ds(pl.multiple_of(o * CHUNK, CHUNK), CHUNK)

    def scatter(src, dst, ss, rs, to, sender):
        return rc(src.at[part(to)], dst.at[sender], ss.at[to], rs.at[sender], to, b)

    s_out[...] = g_out[...].astype(BF16)
    s_log[...] = g_log[...].astype(BF16)

    def send_first(o):
        @pl.when(o < owners)
        def _():
            scatter(s_out, r_out, ros, ror, o, t).start()

        @pl.when(o < log_chunks)
        def _():
            scatter(s_log, r_log, rls, rlr, o, t).start()

    peers(send_first)

    for k in slots:
        if not (chained and k == far):
            @pl.when(gets_bwd(k))
            def _(k=k):
                bwd(k).wait_recv()

            @pl.when(jnp.logical_not(gets_bwd(k)))
            def _(k=k):
                cin[k] = jnp.zeros_like(cin[k])

    def finish_values(r):
        total = (low(r, 0) * dmix[r].astype(F32)).astype(BF16).astype(F32)
        for k in slots:
            if not (chained and k == far):
                total = total + cin[k, r].astype(F32)
        dv = total.astype(BF16)
        val[r] = dv
        g_val[...] += dot(dv, feats[0, r])

    for k in order:
        @pl.when(sends_fwd(k))
        def _(k=k):
            fwd(k).wait_send()

    loop(finish_values)
    s_val[...] = g_val[...].astype(BF16)

    def send_second(o):
        @pl.when(o < owners)
        def _():
            scatter(s_val, r_val, rvs, rvr, o, t).start()

    peers(send_second)

    def finish_feats(r):
        g = dot(w_value[...], val[r]) + dot(wl[...], dlog[r])
        out_feats[0, r] = (cot[0, r].astype(F32) + g.T).astype(BF16)

    loop(finish_feats)

    @pl.when(t < owners)
    def _():
        def reduce_one(src, got, rs, at):
            def body(i, total):
                p = lax.rem(t + i, nt)
                rc(got.at[p], got.at[p], rs.at[p], rs.at[p], p, b).wait_recv()
                return total + got[p].astype(F32)

            total = lax.fori_loop(1, nt, body, src[part(t), :])
            band_part[b, at] = total.astype(BF16)

        reduce_one(g_out, r_out, ror, 0)
        reduce_one(g_val, r_val, rvr, 1)

        @pl.when(t < log_chunks)
        def _():
            reduce_one(g_log, r_log, rlr, 2)

        @pl.when(t >= log_chunks)
        def _():
            band_part[b, 2] = jnp.zeros((CHUNK, chans), BF16)

        def swap(i):
            to = lax.rem(b + i, nb)
            return rc(band_part.at[b], band_part.at[b], xs.at[to], xr.at[b], t, to)

        def got(i):
            frm = lax.rem(b + i, nb)
            return rc(band_part.at[frm], band_part.at[frm], xs.at[frm], xr.at[frm], t, frm)

        def start(i, c):
            swap(i).start()
            return c

        def finish(i, c):
            got(i).wait_recv()
            return c

        lax.fori_loop(1, nb, start, 0)
        lax.fori_loop(1, nb, finish, 0)
        total = band_part[0].astype(F32)
        for i in range(1, nb):
            total = total + band_part[i].astype(F32)
        whole[...] = total.astype(BF16)
        gathered[t] = whole[...]

        def spread(p):
            rc(whole.at[pl.ds(0, 2)], gathered.at[t, pl.ds(0, 2)], gs.at[p], gr.at[t], p, b).start()

            @pl.when(t < log_chunks)
            def _():
                rc(whole.at[2], gathered.at[t, 2], gls.at[p], glr.at[t], p, b).start()

        peers(spread)

        def swapped(i, c):
            swap(i).wait_send()
            return c

        lax.fori_loop(1, nb, swapped, 0)

    def collect(p):
        @pl.when(p < owners)
        def _():
            rc(whole.at[pl.ds(0, 2)], gathered.at[p, pl.ds(0, 2)], gs.at[p], gr.at[p], p, b).wait_recv()

        @pl.when(p < log_chunks)
        def _():
            rc(whole.at[2], gathered.at[p, 2], gls.at[p], glr.at[p], p, b).wait_recv()

    peers(collect)

    for o in range(owners):
        out_wout[o * CHUNK : (o + 1) * CHUNK, :] = gathered[o, 0].astype(F32)
        g_val[o * CHUNK : (o + 1) * CHUNK, :] = gathered[o, 1].astype(F32)
    for o in range(log_chunks):
        out_logit[o * CHUNK : (o + 1) * CHUNK, :] = gathered[o, 2].astype(F32)
    out_value[...] = g_val[...].T

    def drain(p):
        @pl.when(p < owners)
        def _():
            scatter(s_out, r_out, ros, ror, p, t).wait_send()
            scatter(s_val, r_val, rvs, rvr, p, t).wait_send()

        @pl.when(p < log_chunks)
        def _():
            scatter(s_log, r_log, rls, rlr, p, t).wait_send()

        @pl.when(t < owners)
        def _():
            rc(whole.at[pl.ds(0, 2)], gathered.at[t, pl.ds(0, 2)], gs.at[p], gr.at[t], p, b).wait_send()

        @pl.when(t < log_chunks)
        def _():
            rc(whole.at[2], gathered.at[t, 2], gls.at[p], glr.at[t], p, b).wait_send()

    peers(drain)
    for k in slots:
        if chained and k == far:
            @pl.when(sends_fwd(k))
            def _(k=k):
                fwd(k).wait_send()

        @pl.when(sends_bwd(k))
        def _(k=k):
            bwd(k).wait_send()

        for side in (0, 1):
            @pl.when(has(side))
            def _(k=k, side=side):
                rim(k, side).wait_send()

            @pl.when((t >= DISTANCES[k]) & has(side))
            def _(k=k, side=side):
                halo(k, side).wait_send()


def shards(nt, nb, feats, cotangent, w_value, w_logit, w_out, row_offsets, col_offsets, fractions, present):
    rows, cols, chans = feats.shape[1:]
    owners = chans // CHUNK
    wl = w_logit.reshape(chans, H, J).transpose(0, 2, 1).reshape(chans, H * J)
    vmem = pl.BlockSpec(memory_space=pltpu.VMEM)
    slots = sum(1 for d in DISTANCES if d < nt)
    grid = (rows, chans, cols)
    dma = pltpu.SemaphoreType.DMA
    v = pltpu.VMEM
    square = (chans, chans)
    logs = (H * J, chans)
    landing = (nt, CHUNK, chans)
    scratch = [
        v(grid, BF16),
        v((slots, rows + 2, chans, cols), BF16),
        v((slots, rows, 3 * cols, cols), BF16),
        v((rows, slots + 1, H, cols), F32),
        v(grid, BF16),
        v((rows, slots + 1, H, cols), F32),
        v(grid, F32),
        v((rows, H * J, cols), BF16),
        v((slots, rows + 2, chans, cols), F32),
        v((slots,) + grid, BF16),
        v((slots,) + grid, BF16),
        v((slots, 2, chans, cols), BF16),
        v((slots, 2, chans, cols), BF16),
        v(square, F32), v(square, F32), v(logs, F32),
        v(square, BF16), v(square, BF16), v(logs, BF16),
        v(landing, BF16), v(landing, BF16), v(landing, BF16),
        v((nb, 3, CHUNK, chans), BF16),
        v((3, CHUNK, chans), BF16),
        v((nt, 3, CHUNK, chans), BF16),
        dma((slots,)), dma((slots,)),
        dma((slots, 2)), dma((slots, 2)),
        dma((slots,)), dma((slots,)),
        dma((slots, 2)), dma((slots, 2)),
        dma((nt,)), dma((nt,)), dma((nt,)), dma((nt,)), dma((nt,)), dma((nt,)),
        dma((nb,)), dma((nb,)),
        dma((nt,)), dma((nt,)), dma((nt,)), dma((nt,)),
    ]
    grad_feats, g_value, g_logit, g_out = pl.pallas_call(
        functools.partial(kernel, nt, nb, owners),
        out_shape=(
            jax.ShapeDtypeStruct(feats.shape, BF16),
            jax.ShapeDtypeStruct(square, F32),
            jax.ShapeDtypeStruct(logs, F32),
            jax.ShapeDtypeStruct(square, F32),
        ),
        in_specs=[vmem] * 10 + [pl.BlockSpec(memory_space=pltpu.SMEM)],
        out_specs=(vmem,) * 4,
        scratch_shapes=scratch,
        compiler_params=pltpu.CompilerParams(
            collective_id=0, has_side_effects=True, vmem_limit_bytes=56 * 1024 * 1024
        ),
    )(feats, cotangent, w_value, w_value.T, w_out, wl.T, wl, row_offsets, col_offsets, fractions, present)
    g_logit = g_logit.reshape(J, H, chans).transpose(2, 1, 0).reshape(chans, H * J)
    return grad_feats, g_value, g_logit, g_out


def solution(mesh):
    placed = (
        P("tm", "band", None, None),
        P("tm", "band", None, None),
        P(),
        P(),
        P(),
        P("tm", None, "band", None),
        P("tm", None, "band", None),
        P("tm", None, None, "band", None),
        P("tm", None),
    )
    return jax.shard_map(
        functools.partial(shards, mesh.shape["tm"], mesh.shape["band"]),
        mesh=mesh,
        in_specs=placed,
        out_specs=(P("tm", "band", None, None), P(), P(), P()),
        check_vma=False,
    )
```

```python
import functools

import jax
import jax.numpy as jnp
from jax import lax
from jax.experimental import pallas as pl
from jax.experimental.pallas import tpu as pltpu
from jax.sharding import PartitionSpec as P

H = 8
E = 32
K = 5
J = 6
DISTANCES = (1, 2, 4, 8, 16)
CHUNK = 16
MESH = pl.DeviceIdType.MESH
F32 = jnp.float32
BF16 = jnp.bfloat16


def nt_dot(a, b):
    return lax.dot_general(a, b, (((1,), (1,)), ((), ())), preferred_element_type=F32)


def dot(a, b):
    return jnp.dot(a, b, preferred_element_type=F32)


def entry_order(axis):
    mine = lax.broadcasted_iota(jnp.int32, (H * J, H * J), axis)
    theirs = lax.broadcasted_iota(jnp.int32, (H * J, H * J), 1 - axis)
    return jnp.where(theirs == (mine & (H - 1)) * J + (mine >> 3), F32(1.0), F32(0.0)).astype(BF16)


def spread_heads(a):
    return jnp.concatenate([jnp.broadcast_to(a[h : h + 1], (E, a.shape[1])) for h in range(H)], axis=0)


def head_sums(x):
    return jnp.sum(x.reshape(H, E, x.shape[1]), axis=1)


def kernel(
    nt, nb, owners,
    feats, cot, w_value, w_logit, w_out, row_off, col_off, frac, present,
    out_feats, out_sums, out_logs,
    w_value_t, wl_t, wl, val, ext, tables, attn, dmix, dattn, mix, dlog, dval, acc, cout, cin, rim_out, rim_in,
    g_out, g_val, g_log, s_out, s_val, s_log, r_out, r_val, r_log,
    band_part, whole, gathered,
    fs, fr, hs, hr, bs, br, ms, mr, ros, ror, rvs, rvr, rls, rlr, xs, xr, gs, gr, gls, glr,
):
    t = lax.axis_index("tm")
    b = lax.axis_index("band")
    rows, cols, chans = feats.shape[1:]
    slots = [k for k in range(K) if DISTANCES[k] < nt]
    chained = 2 in slots and 3 in slots
    near, far = 2, 3
    log_chunks = (H * J) // CHUNK

    barrier = pltpu.get_barrier_semaphore()

    def greet_t(i, c):
        pl.semaphore_signal(barrier, inc=1, device_id=(lax.rem(t + i, nt), b), device_id_type=MESH)
        return c

    def greet_b(i, c):
        pl.semaphore_signal(barrier, inc=1, device_id=(t, lax.rem(b + i, nb)), device_id_type=MESH)
        return c

    lax.fori_loop(1, nt, greet_t, 0)
    lax.fori_loop(1, nb, greet_b, 0)

    def rc(src, dst, ss, rs, tt, bb):
        return pltpu.make_async_remote_copy(
            src_ref=src, dst_ref=dst, send_sem=ss, recv_sem=rs, device_id=(tt, bb), device_id_type=MESH
        )

    def loop(body):
        for r in range(rows):
            body(r)

    def pairs(body):
        for p in range(rows // 2):
            body(p, slice(2 * p * cols, (2 * p + 2) * cols))

    def cells(ref, p):
        return ref[0, 2 * p : 2 * p + 2].reshape(2 * cols, chans)

    w_value_t[...] = w_value[...].astype(F32).T.astype(BF16)
    order_in = entry_order(0)
    wl_t[...] = nt_dot(order_in, w_logit[...]).astype(BF16)
    wl[...] = nt_dot(w_logit[...], order_in).astype(BF16)

    def make_values(p, at):
        v = nt_dot(w_value_t[...], cells(feats, p)).astype(BF16)
        val[2 * p] = v[:, :cols]
        val[2 * p + 1] = v[:, cols:]

    pairs(make_values)
    pl.semaphore_wait(barrier, nt - 1 + nb - 1)

    def hop(k):
        return DISTANCES[near] if chained and k == far else DISTANCES[k]

    def main_of(k):
        return ext.at[k, pl.ds(1, rows)]

    def fwd(k):
        src = main_of(near) if chained and k == far else val
        return rc(src, main_of(k), fs.at[k], fr.at[k], lax.rem(t + hop(k), nt), b)

    def sends_fwd(k):
        if chained and k == far:
            return (t >= DISTANCES[near]) & (t + DISTANCES[near] < nt)
        return t + DISTANCES[k] < nt

    order = [k for k in (2, 1, 0, 4) if k in slots]
    for k in order:
        @pl.when(sends_fwd(k))
        def _(k=k):
            fwd(k).start()

    def make_attn(p, at):
        dmix[:, at] = nt_dot(w_out[...], cells(cot, p)).astype(BF16)
        logits = nt_dot(wl_t[...], cells(feats, p))
        ls = [logits[0:H]]
        oks = [None]
        for k in slots:
            flag = present[0, k] * jnp.where(t >= DISTANCES[k], 1, 0)
            ok = jnp.full((H, 2 * cols), flag, jnp.int32) == 1
            oks.append(ok)
            ls.append(jnp.where(ok, logits[H * (k + 1) : H * (k + 2)], F32(-1e30)))
        top = functools.reduce(jnp.maximum, ls)
        es = []
        for ok, l in zip(oks, ls):
            e = jnp.exp(l - top)
            es.append(e if ok is None else jnp.where(ok, e, F32(0.0)))
        total = functools.reduce(jnp.add, es)
        for j in range(len(es)):
            attn[j, :, at] = es[j] / total

    pairs(make_attn)

    def low(j, at):
        return spread_heads(attn[j, :, at].astype(BF16).astype(F32))

    def rim(k, side):
        other = b - 1 if side == 0 else b + 1
        return rc(rim_out.at[k, side], rim_in.at[k, 1 - side], ms.at[k, side], mr.at[k, 1 - side],
                  t, lax.rem(other + nb, nb))

    def has(side):
        return b > 0 if side == 0 else b < nb - 1

    def contribute(k):
        delta = lax.broadcasted_iota(jnp.int32, (cols, cols), 0) - lax.broadcasted_iota(jnp.int32, (cols, cols), 1)

        def one_row(r):
            up = row_off[0, k, r : r + 1, :] < 0
            u = delta - col_off[0, k, r : r + 1, :]
            fa = frac[0, 0, k, r : r + 1, :].astype(F32)
            fb = frac[0, 1, k, r : r + 1, :].astype(F32)
            wc = jnp.where(u == 0, 8.0 - fb, jnp.where(u == 1, fb, F32(0.0)))
            first = (8.0 - fa) / 64.0
            second = fa / 64.0
            weights = (jnp.where(up, first, F32(0.0)), jnp.where(up, second, first), jnp.where(up, F32(0.0), second))
            return [(wc * w).astype(BF16) for w in weights]

        empty = jnp.zeros((cols, cols), BF16)

        def body(p, at):
            left = jnp.concatenate(one_row(2 * p) + [empty], axis=0)
            right = jnp.concatenate([empty] + one_row(2 * p + 1), axis=0)
            table = jnp.concatenate([left, right], axis=1)
            tables[k, p] = table
            ds = (low(k + 1, at) * dmix[:, at].astype(F32)).astype(BF16)
            part = nt_dot(ds, table)
            for d in range(4):
                piece = part[:, d * cols : (d + 1) * cols]
                if d < 2 and p > 0:
                    acc[k, 2 * p + d] += piece
                else:
                    acc[k, 2 * p + d] = piece

        pairs(body)
        for side in (0, 1):
            rim_out[k, side] = acc[k, 0 if side == 0 else rows + 1].astype(BF16)

            @pl.when(has(side))
            def _(side=side):
                rim(k, side).start()

    def bwd(k):
        return rc(cout.at[k], cin.at[k], bs.at[k], br.at[k], lax.rem(t - hop(k) + nt, nt), b)

    def sends_bwd(k):
        return t >= DISTANCES[k]

    def gets_bwd(k):
        if chained and k == far:
            return (t >= DISTANCES[near]) & (t + DISTANCES[near] < nt)
        return t + DISTANCES[k] < nt

    def finish_contribution(k):
        for side in (0, 1):
            @pl.when(has(side))
            def _(side=side):
                rim(k, 1 - side).wait_recv()
                row = 1 if side == 0 else rows
                acc[k, row] += rim_in[k, side].astype(F32)

        if chained and k == near:
            @pl.when(gets_bwd(far))
            def _():
                bwd(far).wait_recv()

                def body(r):
                    acc[k, r + 1] += cin[far, r].astype(F32)

                loop(body)

        def body(r):
            cout[k, r] = acc[k, r + 1].astype(BF16)

        loop(body)

        @pl.when(sends_bwd(k))
        def _():
            bwd(k).start()

    back_order = [k for k in (3, 1, 0, 2, 4) if k in slots]
    late = [near] if chained else []
    previous = None
    for k in back_order:
        contribute(k)
        if previous is not None:
            finish_contribution(previous)
        previous = None if k in late else k
    if previous is not None:
        finish_contribution(previous)

    def halo(k, side):
        src = ext.at[k, 1 if side == 0 else rows]
        dst = ext.at[k, rows + 1 if side == 0 else 0]
        other = b - 1 if side == 0 else b + 1
        return rc(src, dst, hs.at[k, side], hr.at[k, 1 - side], t, lax.rem(other + nb, nb))

    def take(k):
        @pl.when(t >= DISTANCES[k])
        def _():
            fwd(k).wait_recv()
            for side in (0, 1):
                @pl.when(has(side))
                def _(side=side):
                    halo(k, side).start()

                @pl.when(jnp.logical_not(has(side)))
                def _(side=side):
                    ext[k, 0 if side == 0 else rows + 1] = jnp.zeros((chans, cols), BF16)

        @pl.when(t < DISTANCES[k])
        def _():
            ext[k] = jnp.zeros_like(ext[k])

    def own_sample(p, at):
        s = jnp.concatenate([val[2 * p], val[2 * p + 1]], axis=1).astype(F32)
        mix[:, at] = low(0, at) * s
        dattn[0, :, at] = head_sums(dmix[:, at].astype(F32) * s)

    def sample(k):
        for side in (0, 1):
            @pl.when((t >= DISTANCES[k]) & has(side))
            def _(side=side):
                halo(k, 1 - side).wait_recv()

        def body(p, at):
            v = jnp.concatenate([ext[k, 2 * p + d] for d in range(4)], axis=1)
            s = dot(v, tables[k, p]).astype(BF16).astype(F32)
            mix[:, at] += low(k + 1, at) * s
            dattn[k + 1, :, at] = head_sums(dmix[:, at].astype(F32) * s)

        pairs(body)

    if chained:
        take(near)

        @pl.when(sends_fwd(far))
        def _():
            fwd(far).start()

    pairs(own_sample)
    for k in order:
        if not (chained and k == near):
            take(k)
    for k in late:
        finish_contribution(k)
    for k in order:
        sample(k)
    if far in slots:
        take(far)
        sample(far)

    used = len(slots) + 1

    def finish_attn(p, at):
        ats = [attn[j, :, at] for j in range(used)]
        das = [dattn[j, :, at] for j in range(used)]
        inner = functools.reduce(jnp.add, [a * d for a, d in zip(ats, das)])
        dls = [a * (d - inner) for a, d in zip(ats, das)]
        dls += [jnp.zeros((H, 2 * cols), F32)] * (J - used)
        dlog[:, at] = jnp.concatenate(dls, axis=0).astype(BF16)

    pairs(finish_attn)

    def all_cells(ref):
        return ref[0].reshape(rows * cols, chans)

    g_log[...] = dot(dlog[...], all_cells(feats))
    g_out[...] = dot(mix[...].astype(BF16), all_cells(cot))

    def peers(body):
        def step(i, c):
            body(lax.rem(t + i, nt))
            return c

        lax.fori_loop(1, nt, step, 0)

    def part(o):
        return pl.ds(pl.multiple_of(o * CHUNK, CHUNK), CHUNK)

    def scatter(src, dst, ss, rs, to, sender):
        return rc(src.at[part(to)], dst.at[sender], ss.at[to], rs.at[sender], to, b)

    s_out[...] = g_out[...].astype(BF16)
    s_log[...] = g_log[...].astype(BF16)

    def send_first(o):
        @pl.when(o < owners)
        def _():
            scatter(s_out, r_out, ros, ror, o, t).start()

        @pl.when(o < log_chunks)
        def _():
            scatter(s_log, r_log, rls, rlr, o, t).start()

    peers(send_first)

    for k in slots:
        if not (chained and k == far):
            @pl.when(gets_bwd(k))
            def _(k=k):
                bwd(k).wait_recv()

            @pl.when(jnp.logical_not(gets_bwd(k)))
            def _(k=k):
                cin[k] = jnp.zeros_like(cin[k])

    def finish_values(p, at):
        total = (low(0, at) * dmix[:, at].astype(F32)).astype(BF16).astype(F32)
        for k in slots:
            if not (chained and k == far):
                total = total + jnp.concatenate([cin[k, 2 * p], cin[k, 2 * p + 1]], axis=1).astype(F32)
        dval[:, at] = total.astype(BF16)

    for k in order:
        @pl.when(sends_fwd(k))
        def _(k=k):
            fwd(k).wait_send()

    pairs(finish_values)
    g_val[...] = dot(dval[...], all_cells(feats))
    s_val[...] = g_val[...].astype(BF16)

    def send_second(o):
        @pl.when(o < owners)
        def _():
            scatter(s_val, r_val, rvs, rvr, o, t).start()

    peers(send_second)

    def finish_feats(p, at):
        g = dot(w_value[...], dval[:, at]) + dot(wl[...], dlog[:, at])
        done = (cells(cot, p).astype(F32) + g.T).astype(BF16)
        out_feats[0, 2 * p : 2 * p + 2] = done.reshape(2, cols, chans)

    pairs(finish_feats)

    @pl.when(t < owners)
    def _():
        def reduce_one(src, got, rs, at):
            def body(i, total):
                p = lax.rem(t + i, nt)
                rc(got.at[p], got.at[p], rs.at[p], rs.at[p], p, b).wait_recv()
                return total + got[p].astype(F32)

            total = lax.fori_loop(1, nt, body, src[part(t), :])
            band_part[b, at] = total.astype(BF16)

        reduce_one(g_out, r_out, ror, 0)
        reduce_one(g_val, r_val, rvr, 1)

        @pl.when(t < log_chunks)
        def _():
            reduce_one(g_log, r_log, rlr, 2)

        @pl.when(t >= log_chunks)
        def _():
            band_part[b, 2] = jnp.zeros((CHUNK, chans), BF16)

        def swap(i):
            to = lax.rem(b + i, nb)
            return rc(band_part.at[b], band_part.at[b], xs.at[to], xr.at[b], t, to)

        def got(i):
            frm = lax.rem(b + i, nb)
            return rc(band_part.at[frm], band_part.at[frm], xs.at[frm], xr.at[frm], t, frm)

        def start(i, c):
            swap(i).start()
            return c

        def finish(i, c):
            got(i).wait_recv()
            return c

        lax.fori_loop(1, nb, start, 0)
        lax.fori_loop(1, nb, finish, 0)
        total = band_part[0].astype(F32)
        for i in range(1, nb):
            total = total + band_part[i].astype(F32)
        whole[...] = total.astype(BF16)
        gathered[t] = whole[...]

        def spread(p):
            rc(whole.at[pl.ds(0, 2)], gathered.at[t, pl.ds(0, 2)], gs.at[p], gr.at[t], p, b).start()

            @pl.when(t < log_chunks)
            def _():
                rc(whole.at[2], gathered.at[t, 2], gls.at[p], glr.at[t], p, b).start()

        peers(spread)

        def swapped(i, c):
            swap(i).wait_send()
            return c

        lax.fori_loop(1, nb, swapped, 0)

    def collect(p):
        @pl.when(p < owners)
        def _():
            rc(whole.at[pl.ds(0, 2)], gathered.at[p, pl.ds(0, 2)], gs.at[p], gr.at[p], p, b).wait_recv()

        @pl.when(p < log_chunks)
        def _():
            rc(whole.at[2], gathered.at[p, 2], gls.at[p], glr.at[p], p, b).wait_recv()

    peers(collect)

    for i in (0, 1):
        out_sums[i] = gathered[:owners, i].reshape(chans, chans)
    out_logs[...] = gathered[:log_chunks, 2].reshape(H * J, chans)

    def drain(p):
        @pl.when(p < owners)
        def _():
            scatter(s_out, r_out, ros, ror, p, t).wait_send()
            scatter(s_val, r_val, rvs, rvr, p, t).wait_send()

        @pl.when(p < log_chunks)
        def _():
            scatter(s_log, r_log, rls, rlr, p, t).wait_send()

        @pl.when(t < owners)
        def _():
            rc(whole.at[pl.ds(0, 2)], gathered.at[t, pl.ds(0, 2)], gs.at[p], gr.at[t], p, b).wait_send()

        @pl.when(t < log_chunks)
        def _():
            rc(whole.at[2], gathered.at[t, 2], gls.at[p], glr.at[t], p, b).wait_send()

    peers(drain)
    for k in slots:
        if chained and k == far:
            @pl.when(sends_fwd(k))
            def _(k=k):
                fwd(k).wait_send()

        @pl.when(sends_bwd(k))
        def _(k=k):
            bwd(k).wait_send()

        for side in (0, 1):
            @pl.when(has(side))
            def _(k=k, side=side):
                rim(k, side).wait_send()

            @pl.when((t >= DISTANCES[k]) & has(side))
            def _(k=k, side=side):
                halo(k, side).wait_send()


def unpack(feats, sums, logs, out_feats, out_value, out_logit, out_wout):
    out_feats[...] = feats[...]
    out_wout[...] = sums[0].astype(F32)
    out_value[...] = sums[1].astype(F32).T
    out_logit[...] = dot(entry_order(1), logs[...]).T


def shards(nt, nb, feats, cotangent, w_value, w_logit, w_out, row_offsets, col_offsets, fractions, present):
    rows, cols, chans = feats.shape[1:]
    owners = chans // CHUNK
    vmem = pl.BlockSpec(memory_space=pltpu.VMEM)
    slots = sum(1 for d in DISTANCES if d < nt)
    grid = (rows, chans, cols)
    dma = pltpu.SemaphoreType.DMA
    v = pltpu.VMEM
    square = (chans, chans)
    logs = (H * J, chans)
    landing = (nt, CHUNK, chans)
    flat = (chans, rows * cols)
    scratch = [
        v(square, BF16), v(logs, BF16), v(logs[::-1], BF16),
        v(grid, BF16),
        v((slots, rows + 2, chans, cols), BF16),
        v((slots, rows // 2, 4 * cols, 2 * cols), BF16),
        v((slots + 1, H, rows * cols), F32),
        v(flat, BF16),
        v((slots + 1, H, rows * cols), F32),
        v(flat, F32),
        v((H * J, rows * cols), BF16),
        v(flat, BF16),
        v((slots, rows + 2, chans, cols), F32),
        v((slots,) + grid, BF16),
        v((slots,) + grid, BF16),
        v((slots, 2, chans, cols), BF16),
        v((slots, 2, chans, cols), BF16),
        v(square, F32), v(square, F32), v(logs, F32),
        v(square, BF16), v(square, BF16), v(logs, BF16),
        v(landing, BF16), v(landing, BF16), v(landing, BF16),
        v((nb, 3, CHUNK, chans), BF16),
        v((3, CHUNK, chans), BF16),
        v((nt, 3, CHUNK, chans), BF16),
        dma((slots,)), dma((slots,)),
        dma((slots, 2)), dma((slots, 2)),
        dma((slots,)), dma((slots,)),
        dma((slots, 2)), dma((slots, 2)),
        dma((nt,)), dma((nt,)), dma((nt,)), dma((nt,)), dma((nt,)), dma((nt,)),
        dma((nb,)), dma((nb,)),
        dma((nt,)), dma((nt,)), dma((nt,)), dma((nt,)),
    ]
    grad_feats, sums, log_sums = pl.pallas_call(
        functools.partial(kernel, nt, nb, owners),
        out_shape=tuple(jax.ShapeDtypeStruct(shape, BF16) for shape in (feats.shape, (2,) + square, logs)),
        in_specs=[vmem] * 8 + [pl.BlockSpec(memory_space=pltpu.SMEM)],
        out_specs=(vmem,) * 3,
        scratch_shapes=scratch,
        compiler_params=pltpu.CompilerParams(
            collective_id=0, has_side_effects=True, vmem_limit_bytes=56 * 1024 * 1024
        ),
    )(feats, cotangent, w_value, w_logit, w_out, row_offsets, col_offsets, fractions, present)
    return pl.pallas_call(
        unpack,
        out_shape=(
            jax.ShapeDtypeStruct(feats.shape, BF16),
            jax.ShapeDtypeStruct(square, F32),
            jax.ShapeDtypeStruct(w_logit.shape, F32),
            jax.ShapeDtypeStruct(square, F32),
        ),
        in_specs=[vmem] * 3,
        out_specs=(vmem,) * 4,
    )(grad_feats, sums, log_sums)


def solution(mesh):
    placed = (
        P("tm", "band", None, None),
        P("tm", "band", None, None),
        P(),
        P(),
        P(),
        P("tm", None, "band", None),
        P("tm", None, "band", None),
        P("tm", None, None, "band", None),
        P("tm", None),
    )
    return jax.shard_map(
        functools.partial(shards, mesh.shape["tm"], mesh.shape["band"]),
        mesh=mesh,
        in_specs=placed,
        out_specs=(P("tm", "band", None, None), P(), P(), P()),
        check_vma=False,
    )
```

```python
import functools

import jax
import jax.numpy as jnp
from jax import lax
from jax.experimental import pallas as pl
from jax.experimental.pallas import tpu as pltpu
from jax.sharding import PartitionSpec as P

H = 8
E = 32
K = 5
J = 6
DISTANCES = (1, 2, 4, 8, 16)
CHUNK = 16
MESH = pl.DeviceIdType.MESH
F32 = jnp.float32
BF16 = jnp.bfloat16


def nt_dot(a, b):
    return lax.dot_general(a, b, (((1,), (1,)), ((), ())), preferred_element_type=F32)


def dot(a, b):
    return jnp.dot(a, b, preferred_element_type=F32)


def entry_order(axis):
    mine = lax.broadcasted_iota(jnp.int32, (H * J, H * J), axis)
    theirs = lax.broadcasted_iota(jnp.int32, (H * J, H * J), 1 - axis)
    return jnp.where(theirs == (mine & (H - 1)) * J + (mine >> 3), F32(1.0), F32(0.0)).astype(BF16)


def spread_heads(a):
    return jnp.concatenate([jnp.broadcast_to(a[h : h + 1], (E, a.shape[1])) for h in range(H)], axis=0)


def head_sums(x):
    return jnp.sum(x.reshape(H, E, x.shape[1]), axis=1)


def kernel(
    nt, nb, owners,
    feats, cot, w_value, w_logit, w_out, row_off, col_off, frac, present,
    out_feats, out_sums, out_logs,
    w_value_t, wl_t, wl, val, ext, tables, attn, dmix, dattn, mix, dlog, dval, acc, cout, cin, rim_out, rim_in,
    g_out, g_val, g_log, s_out, s_val, s_log, r_out, r_val, r_log,
    band_part, whole, gathered,
    fs, fr, hs, hr, bs, br, ms, mr, ros, ror, rvs, rvr, rls, rlr, xs, xr, gs, gr, gls, glr,
    din, ds_sem, das_sem, dar_sem,
):
    t = lax.axis_index("tm")
    b = lax.axis_index("band")
    rows, cols, chans = feats.shape[1:]
    slots = [k for k in range(K) if DISTANCES[k] < nt]
    chained = 2 in slots and 3 in slots
    near, far = 2, 3
    step = DISTANCES[near]
    detours = [k for k in (1, 0) if chained and nt % step == 0]
    log_chunks = (H * J) // CHUNK

    barrier = pltpu.get_barrier_semaphore()

    def greet_t(i, c):
        pl.semaphore_signal(barrier, inc=1, device_id=(lax.rem(t + i, nt), b), device_id_type=MESH)
        return c

    def greet_b(i, c):
        pl.semaphore_signal(barrier, inc=1, device_id=(t, lax.rem(b + i, nb)), device_id_type=MESH)
        return c

    lax.fori_loop(1, nt, greet_t, 0)
    lax.fori_loop(1, nb, greet_b, 0)

    def rc(src, dst, ss, rs, tt, bb):
        return pltpu.make_async_remote_copy(
            src_ref=src, dst_ref=dst, send_sem=ss, recv_sem=rs, device_id=(tt, bb), device_id_type=MESH
        )

    def loop(body):
        for r in range(rows):
            body(r)

    def pairs(body):
        for p in range(rows // 2):
            body(p, slice(2 * p * cols, (2 * p + 2) * cols))

    def cells(ref, p):
        return ref[0, 2 * p : 2 * p + 2].reshape(2 * cols, chans)

    w_value_t[...] = w_value[...].astype(F32).T.astype(BF16)
    order_in = entry_order(0)
    ordered = dot(order_in, w_logit[...])
    wl_t[...] = ordered.astype(BF16)
    wl[...] = ordered.T.astype(BF16)

    def make_values(p, at):
        v = nt_dot(w_value_t[...], cells(feats, p)).astype(BF16)
        val[2 * p] = v[:, :cols]
        val[2 * p + 1] = v[:, cols:]

    pairs(make_values)
    pl.semaphore_wait(barrier, nt - 1 + nb - 1)

    def hop(k):
        return DISTANCES[near] if chained and k == far else DISTANCES[k]

    def main_of(k):
        return ext.at[k, pl.ds(1, rows)]

    def fwd(k):
        src = main_of(near) if chained and k == far else val
        return rc(src, main_of(k), fs.at[k], fr.at[k], lax.rem(t + hop(k), nt), b)

    def sends_fwd(k):
        if chained and k == far:
            return (t >= DISTANCES[near]) & (t + DISTANCES[near] < nt)
        ok = t + DISTANCES[k] < nt
        return ok & (lax.rem(t + DISTANCES[k], step) >= DISTANCES[k]) if k in detours else ok

    def relays(k):
        return (t >= step) & (lax.rem(t, step) + DISTANCES[k] >= step)

    def relay(k):
        to = lax.rem(t + DISTANCES[k] - step + nt, nt)
        return rc(main_of(near), main_of(k), ds_sem.at[k], fr.at[k], to, b)

    def goes_around(k):
        return (t >= DISTANCES[k]) & (lax.rem(t, step) < DISTANCES[k])

    def around(k):
        to = lax.rem(t + step - DISTANCES[k], nt)
        return rc(cout.at[k], din.at[k], das_sem.at[k], dar_sem.at[k], to, b)

    order = [k for k in (2, 1, 0, 4) if k in slots]
    for k in order:
        @pl.when(sends_fwd(k))
        def _(k=k):
            fwd(k).start()

    def make_attn(p, at):
        dmix[:, at] = nt_dot(w_out[...], cells(cot, p)).astype(BF16)
        logits = nt_dot(wl_t[...], cells(feats, p))
        ls = [logits[0:H]]
        oks = [None]
        for k in slots:
            flag = present[0, k] * jnp.where(t >= DISTANCES[k], 1, 0)
            ok = jnp.full((H, 2 * cols), flag, jnp.int32) == 1
            oks.append(ok)
            ls.append(jnp.where(ok, logits[H * (k + 1) : H * (k + 2)], F32(-1e30)))
        top = functools.reduce(jnp.maximum, ls)
        es = []
        for ok, l in zip(oks, ls):
            e = jnp.exp(l - top)
            es.append(e if ok is None else jnp.where(ok, e, F32(0.0)))
        total = functools.reduce(jnp.add, es)
        for j in range(len(es)):
            attn[j, :, at] = es[j] / total

    pairs(make_attn)

    def low(j, at):
        return spread_heads(attn[j, :, at].astype(BF16).astype(F32))

    def rim(k, side):
        other = b - 1 if side == 0 else b + 1
        return rc(rim_out.at[k, side], rim_in.at[k, 1 - side], ms.at[k, side], mr.at[k, 1 - side],
                  t, lax.rem(other + nb, nb))

    def has(side):
        return b > 0 if side == 0 else b < nb - 1

    def contribute(k):
        delta = lax.broadcasted_iota(jnp.int32, (cols, cols), 0) - lax.broadcasted_iota(jnp.int32, (cols, cols), 1)

        def one_row(r):
            up = row_off[0, k, r : r + 1, :] < 0
            u = delta - col_off[0, k, r : r + 1, :]
            fa = frac[0, 0, k, r : r + 1, :].astype(F32)
            fb = frac[0, 1, k, r : r + 1, :].astype(F32)
            wc = jnp.where(u == 0, 8.0 - fb, jnp.where(u == 1, fb, F32(0.0)))
            first = (8.0 - fa) / 64.0
            second = fa / 64.0
            weights = (jnp.where(up, first, F32(0.0)), jnp.where(up, second, first), jnp.where(up, F32(0.0), second))
            return [(wc * w).astype(BF16) for w in weights]

        empty = jnp.zeros((cols, cols), BF16)

        def body(p, at):
            left = jnp.concatenate(one_row(2 * p) + [empty], axis=0)
            right = jnp.concatenate([empty] + one_row(2 * p + 1), axis=0)
            table = jnp.concatenate([left, right], axis=1)
            tables[k, p] = table
            ds = (low(k + 1, at) * dmix[:, at].astype(F32)).astype(BF16)
            part = nt_dot(ds, table)
            for d in range(4):
                piece = part[:, d * cols : (d + 1) * cols]
                if d < 2 and p > 0:
                    acc[k, 2 * p + d] += piece
                else:
                    acc[k, 2 * p + d] = piece

        pairs(body)
        for side in (0, 1):
            rim_out[k, side] = acc[k, 0 if side == 0 else rows + 1].astype(BF16)

            @pl.when(has(side))
            def _(side=side):
                rim(k, side).start()

    def bwd(k):
        return rc(cout.at[k], cin.at[k], bs.at[k], br.at[k], lax.rem(t - hop(k) + nt, nt), b)

    def sends_bwd(k):
        ok = t >= DISTANCES[k]
        return ok & (lax.rem(t, step) >= DISTANCES[k]) if k in detours else ok

    def gets_bwd(k):
        if chained and k == far:
            return (t >= DISTANCES[near]) & (t + DISTANCES[near] < nt)
        ok = t + DISTANCES[k] < nt
        return ok & (lax.rem(t + DISTANCES[k], step) >= DISTANCES[k]) if k in detours else ok

    def finish_contribution(k):
        for side in (0, 1):
            @pl.when(has(side))
            def _(side=side):
                rim(k, 1 - side).wait_recv()
                row = 1 if side == 0 else rows
                acc[k, row] += rim_in[k, side].astype(F32)

        if chained and k == near:
            @pl.when(gets_bwd(far))
            def _():
                bwd(far).wait_recv()

                def body(r):
                    acc[k, r + 1] += cin[far, r].astype(F32)

                loop(body)

        if k == near:
            for n in detours:
                @pl.when(relays(n))
                def _(n=n):
                    around(n).wait_recv()

                    def add(r):
                        acc[k, r + 1] += din[n, r].astype(F32)

                    loop(add)

        def body(r):
            cout[k, r] = acc[k, r + 1].astype(BF16)

        loop(body)

        @pl.when(sends_bwd(k))
        def _():
            bwd(k).start()

        if k in detours:
            @pl.when(goes_around(k))
            def _():
                around(k).start()

    back_order = [k for k in (3, 1, 0, 2, 4) if k in slots]
    late = [near] if chained else []
    previous = None
    for k in back_order:
        contribute(k)
        if previous is not None:
            finish_contribution(previous)
        previous = None if k in late else k
    if previous is not None:
        finish_contribution(previous)

    def halo(k, side):
        src = ext.at[k, 1 if side == 0 else rows]
        dst = ext.at[k, rows + 1 if side == 0 else 0]
        other = b - 1 if side == 0 else b + 1
        return rc(src, dst, hs.at[k, side], hr.at[k, 1 - side], t, lax.rem(other + nb, nb))

    def take(k):
        @pl.when(t >= DISTANCES[k])
        def _():
            fwd(k).wait_recv()
            for side in (0, 1):
                @pl.when(has(side))
                def _(side=side):
                    halo(k, side).start()

                @pl.when(jnp.logical_not(has(side)))
                def _(side=side):
                    ext[k, 0 if side == 0 else rows + 1] = jnp.zeros((chans, cols), BF16)

        @pl.when(t < DISTANCES[k])
        def _():
            ext[k] = jnp.zeros_like(ext[k])

    def own_sample(p, at):
        s = jnp.concatenate([val[2 * p], val[2 * p + 1]], axis=1).astype(F32)
        mix[:, at] = low(0, at) * s
        dattn[0, :, at] = head_sums(dmix[:, at].astype(F32) * s)

    def sample(k):
        for side in (0, 1):
            @pl.when((t >= DISTANCES[k]) & has(side))
            def _(side=side):
                halo(k, 1 - side).wait_recv()

        def body(p, at):
            v = jnp.concatenate([ext[k, 2 * p + d] for d in range(4)], axis=1)
            s = dot(v, tables[k, p]).astype(BF16).astype(F32)
            mix[:, at] += low(k + 1, at) * s
            dattn[k + 1, :, at] = head_sums(dmix[:, at].astype(F32) * s)

        pairs(body)

    if chained:
        take(near)

        @pl.when(sends_fwd(far))
        def _():
            fwd(far).start()

    for k in detours:
        @pl.when(relays(k))
        def _(k=k):
            relay(k).start()

    for k in late:
        finish_contribution(k)
    pairs(own_sample)
    for k in order:
        if not (chained and k == near):
            take(k)
    for k in order:
        sample(k)
    if far in slots:
        take(far)
        sample(far)

    used = len(slots) + 1

    def finish_attn(p, at):
        ats = [attn[j, :, at] for j in range(used)]
        das = [dattn[j, :, at] for j in range(used)]
        inner = functools.reduce(jnp.add, [a * d for a, d in zip(ats, das)])
        dls = [a * (d - inner) for a, d in zip(ats, das)]
        dls += [jnp.zeros((H, 2 * cols), F32)] * (J - used)
        dlog[:, at] = jnp.concatenate(dls, axis=0).astype(BF16)

    pairs(finish_attn)

    def all_cells(ref):
        return ref[0].reshape(rows * cols, chans)

    g_log[...] = dot(dlog[...], all_cells(feats))
    g_out[...] = dot(mix[...].astype(BF16), all_cells(cot))

    def peers(body):
        def step(i, c):
            body(lax.rem(t + i, nt))
            return c

        lax.fori_loop(1, nt, step, 0)

    def part(o):
        return pl.ds(pl.multiple_of(o * CHUNK, CHUNK), CHUNK)

    def scatter(src, dst, ss, rs, to, sender):
        return rc(src.at[part(to)], dst.at[sender], ss.at[to], rs.at[sender], to, b)

    s_out[...] = g_out[...].astype(BF16)
    s_log[...] = g_log[...].astype(BF16)

    def send_first(o):
        @pl.when(o < owners)
        def _():
            scatter(s_out, r_out, ros, ror, o, t).start()

        @pl.when(o < log_chunks)
        def _():
            scatter(s_log, r_log, rls, rlr, o, t).start()

    peers(send_first)

    for k in slots:
        if not (chained and k == far):
            @pl.when(gets_bwd(k))
            def _(k=k):
                bwd(k).wait_recv()

            @pl.when(jnp.logical_not(gets_bwd(k)))
            def _(k=k):
                cin[k] = jnp.zeros_like(cin[k])

    def finish_values(p, at):
        total = (low(0, at) * dmix[:, at].astype(F32)).astype(BF16).astype(F32)
        for k in slots:
            if not (chained and k == far):
                total = total + jnp.concatenate([cin[k, 2 * p], cin[k, 2 * p + 1]], axis=1).astype(F32)
        dval[:, at] = total.astype(BF16)

    for k in order:
        @pl.when(sends_fwd(k))
        def _(k=k):
            fwd(k).wait_send()

    pairs(finish_values)
    g_val[...] = dot(dval[...], all_cells(feats))
    s_val[...] = g_val[...].astype(BF16)

    def send_second(o):
        @pl.when(o < owners)
        def _():
            scatter(s_val, r_val, rvs, rvr, o, t).start()

    peers(send_second)

    def finish_feats(p, at):
        g = dot(w_value[...], dval[:, at]) + dot(wl[...], dlog[:, at])
        done = (cells(cot, p).astype(F32) + g.T).astype(BF16)
        out_feats[0, 2 * p : 2 * p + 2] = done.reshape(2, cols, chans)

    pairs(finish_feats)

    @pl.when(t < owners)
    def _():
        def reduce_one(src, got, rs, at):
            def body(i, total):
                p = lax.rem(t + i, nt)
                rc(got.at[p], got.at[p], rs.at[p], rs.at[p], p, b).wait_recv()
                return total + got[p].astype(F32)

            total = lax.fori_loop(1, nt, body, src[part(t), :])
            band_part[b, at] = total.astype(BF16)

        reduce_one(g_out, r_out, ror, 0)
        reduce_one(g_val, r_val, rvr, 1)

        @pl.when(t < log_chunks)
        def _():
            reduce_one(g_log, r_log, rlr, 2)

        @pl.when(t >= log_chunks)
        def _():
            band_part[b, 2] = jnp.zeros((CHUNK, chans), BF16)

        def swap(i):
            to = lax.rem(b + i, nb)
            return rc(band_part.at[b], band_part.at[b], xs.at[to], xr.at[b], t, to)

        def got(i):
            frm = lax.rem(b + i, nb)
            return rc(band_part.at[frm], band_part.at[frm], xs.at[frm], xr.at[frm], t, frm)

        def start(i, c):
            swap(i).start()
            return c

        def finish(i, c):
            got(i).wait_recv()
            return c

        lax.fori_loop(1, nb, start, 0)
        lax.fori_loop(1, nb, finish, 0)
        total = band_part[0].astype(F32)
        for i in range(1, nb):
            total = total + band_part[i].astype(F32)
        whole[...] = total.astype(BF16)
        gathered[t] = whole[...]

        def spread(p):
            rc(whole.at[pl.ds(0, 2)], gathered.at[t, pl.ds(0, 2)], gs.at[p], gr.at[t], p, b).start()

            @pl.when(t < log_chunks)
            def _():
                rc(whole.at[2], gathered.at[t, 2], gls.at[p], glr.at[t], p, b).start()

        peers(spread)

        def swapped(i, c):
            swap(i).wait_send()
            return c

        lax.fori_loop(1, nb, swapped, 0)

    def collect(p):
        @pl.when(p < owners)
        def _():
            rc(whole.at[pl.ds(0, 2)], gathered.at[p, pl.ds(0, 2)], gs.at[p], gr.at[p], p, b).wait_recv()

        @pl.when(p < log_chunks)
        def _():
            rc(whole.at[2], gathered.at[p, 2], gls.at[p], glr.at[p], p, b).wait_recv()

    peers(collect)

    for i in (0, 1):
        out_sums[i] = gathered[:owners, i].reshape(chans, chans)
    out_logs[...] = gathered[:log_chunks, 2].reshape(H * J, chans)

    def drain(p):
        @pl.when(p < owners)
        def _():
            scatter(s_out, r_out, ros, ror, p, t).wait_send()
            scatter(s_val, r_val, rvs, rvr, p, t).wait_send()

        @pl.when(p < log_chunks)
        def _():
            scatter(s_log, r_log, rls, rlr, p, t).wait_send()

        @pl.when(t < owners)
        def _():
            rc(whole.at[pl.ds(0, 2)], gathered.at[t, pl.ds(0, 2)], gs.at[p], gr.at[t], p, b).wait_send()

        @pl.when(t < log_chunks)
        def _():
            rc(whole.at[2], gathered.at[t, 2], gls.at[p], glr.at[t], p, b).wait_send()

    peers(drain)
    for k in slots:
        if chained and k == far:
            @pl.when(sends_fwd(k))
            def _(k=k):
                fwd(k).wait_send()

        @pl.when(sends_bwd(k))
        def _(k=k):
            bwd(k).wait_send()

        if k in detours:
            @pl.when(relays(k))
            def _(k=k):
                relay(k).wait_send()

            @pl.when(goes_around(k))
            def _(k=k):
                around(k).wait_send()

        for side in (0, 1):
            @pl.when(has(side))
            def _(k=k, side=side):
                rim(k, side).wait_send()

            @pl.when((t >= DISTANCES[k]) & has(side))
            def _(k=k, side=side):
                halo(k, side).wait_send()


def unpack(feats, sums, logs, out_feats, out_value, out_logit, out_wout):
    out_feats[...] = feats[...]
    out_wout[...] = sums[0].astype(F32)
    out_value[...] = sums[1].astype(F32).T
    out_logit[...] = dot(entry_order(1), logs[...])


def shards(nt, nb, feats, cotangent, w_value, w_logit, w_out, row_offsets, col_offsets, fractions, present):
    rows, cols, chans = feats.shape[1:]
    owners = chans // CHUNK
    vmem = pl.BlockSpec(memory_space=pltpu.VMEM)
    slots = sum(1 for d in DISTANCES if d < nt)
    grid = (rows, chans, cols)
    dma = pltpu.SemaphoreType.DMA
    v = pltpu.VMEM
    square = (chans, chans)
    logs = (H * J, chans)
    landing = (nt, CHUNK, chans)
    flat = (chans, rows * cols)
    scratch = [
        v(square, BF16), v(logs, BF16), v(logs[::-1], BF16),
        v(grid, BF16),
        v((slots, rows + 2, chans, cols), BF16),
        v((slots, rows // 2, 4 * cols, 2 * cols), BF16),
        v((slots + 1, H, rows * cols), F32),
        v(flat, BF16),
        v((slots + 1, H, rows * cols), F32),
        v(flat, F32),
        v((H * J, rows * cols), BF16),
        v(flat, BF16),
        v((slots, rows + 2, chans, cols), F32),
        v((slots,) + grid, BF16),
        v((slots,) + grid, BF16),
        v((slots, 2, chans, cols), BF16),
        v((slots, 2, chans, cols), BF16),
        v(square, F32), v(square, F32), v(logs, F32),
        v(square, BF16), v(square, BF16), v(logs, BF16),
        v(landing, BF16), v(landing, BF16), v(landing, BF16),
        v((nb, 3, CHUNK, chans), BF16),
        v((3, CHUNK, chans), BF16),
        v((nt, 3, CHUNK, chans), BF16),
        dma((slots,)), dma((slots,)),
        dma((slots, 2)), dma((slots, 2)),
        dma((slots,)), dma((slots,)),
        dma((slots, 2)), dma((slots, 2)),
        dma((nt,)), dma((nt,)), dma((nt,)), dma((nt,)), dma((nt,)), dma((nt,)),
        dma((nb,)), dma((nb,)),
        dma((nt,)), dma((nt,)), dma((nt,)), dma((nt,)),
        v((2,) + grid, BF16), dma((2,)), dma((2,)), dma((2,)),
    ]
    grad_feats, sums, log_sums = pl.pallas_call(
        functools.partial(kernel, nt, nb, owners),
        out_shape=tuple(jax.ShapeDtypeStruct(shape, BF16) for shape in (feats.shape, (2,) + square, logs)),
        in_specs=[vmem] * 8 + [pl.BlockSpec(memory_space=pltpu.SMEM)],
        out_specs=(vmem,) * 3,
        scratch_shapes=scratch,
        compiler_params=pltpu.CompilerParams(
            collective_id=0, has_side_effects=True, vmem_limit_bytes=56 * 1024 * 1024
        ),
    )(feats, cotangent, w_value, w_logit.T, w_out, row_offsets, col_offsets, fractions, present)
    outs = pl.pallas_call(
        unpack,
        out_shape=(
            jax.ShapeDtypeStruct(feats.shape, BF16),
            jax.ShapeDtypeStruct(square, F32),
            jax.ShapeDtypeStruct(logs, F32),
            jax.ShapeDtypeStruct(square, F32),
        ),
        in_specs=[vmem] * 3,
        out_specs=(vmem,) * 4,
    )(grad_feats, sums, log_sums)
    return outs[0], outs[1], outs[2].T, outs[3]


def solution(mesh):
    placed = (
        P("tm", "band", None, None),
        P("tm", "band", None, None),
        P(),
        P(),
        P(),
        P("tm", None, "band", None),
        P("tm", None, "band", None),
        P("tm", None, None, "band", None),
        P("tm", None),
    )
    return jax.shard_map(
        functools.partial(shards, mesh.shape["tm"], mesh.shape["band"]),
        mesh=mesh,
        in_specs=placed,
        out_specs=(P("tm", "band", None, None), P(), P(), P()),
        check_vma=False,
    )
```
